256 devices in a mesh: dp: 32 (over y, z), mp: 8 (over x, core).
Axes of the slice: x: 4, y: 4, z: 8, core: 2. Of those that a mesh axis runs over, the one named last changes fastest.
Arguments:
- tokens: bfloat16 [4096, 8192], P('dp'), may hold values from -6 to 6
- rotation: float32 [8192, 8192], P('dp', 'mp'), may hold values from -6 to 6
- key_weight: bfloat16 [8192, 1024], P('dp', 'mp'), may hold values from -0.125 to 0.125
- grad_out: bfloat16 [4096, 1024], P('dp', 'mp'), may hold values from -6 to 6
Outputs:
- projected: bfloat16 [4096, 1024], P('dp', 'mp')
- new_panel: float32 [8192, 128], P('dp', 'mp')
The draws below stay inside these ranges and needn't reach their ends.
All inputs are finite; a program needn't handle non-finite values.
Results may differ from the reference program's by a relative error of at most 0.014.
Values may be sent and summed in bfloat16 or wider, within the bound.
No kernel may reach another device: no remote copies, remote signals or barrier semaphores. Data moves between devices by JAX's collectives and lax.ppermute only.
A program may use at most 128 MiB of HBM per device.

```python
import jax
import jax.numpy as jnp
from jax import lax

D = 8192
F = 1024
PANEL = 128
ITERS = 2
TOKENS = 4096


def raised(drawn, own_key, source, target, parts, factor):
    owner, partner = [(jnp.arange(drawn.shape[dim]) // (drawn.shape[dim] // parts)).reshape([-1 if axis == dim else 1 for axis in range(drawn.ndim)]) for dim in (source, target)]
    chosen = jax.random.permutation(own_key, parts)[partner]
    strong = (owner == chosen) | (owner == (partner + parts // 2) % parts)
    return jnp.where(strong, factor * drawn, drawn)


def steps_of(key, extent, pieces, low, high):
    level, own = 1.0, jax.random.fold_in(key, 6)
    for position, shards_of in pieces:
        heights = jnp.exp(jax.random.uniform(jax.random.fold_in(own, position), (shards_of,), jnp.float32, low / len(pieces), high / len(pieces)))
        level = level * jnp.repeat(heights, extent[position] // shards_of).reshape([-1 if axis == position else 1 for axis in range(len(extent))])
    return level


def scatter_about(own_key, shape, deviation, limit, pieces=(), dtype=jnp.bfloat16):
    values = jax.random.normal(own_key, shape, jnp.float32) * deviation
    if len(pieces) > 0:
        values = steps_of(own_key, shape, pieces, -0.22, 0.18) * values
    return jnp.clip(values, min=-limit, max=limit).astype(dtype)


def gaussian_with(own_key, extent, deviation, reach, shards, heavy, held_as=jnp.bfloat16):
    values = deviation * jax.random.normal(own_key, extent, jnp.float32)
    if shards:
        values = values * steps_of(own_key, extent, shards, -0.22, 0.18)
    return jnp.clip(raised(values, jax.random.fold_in(own_key, 3), *heavy), -reach, reach).astype(held_as)


def setup_inputs(seed: int = 0) -> dict:
    splits = jax.random.split(jax.random.key(seed), 5)
    return {
        "tokens": gaussian_with(splits[0], (TOKENS, D), 1.0, 6.0, ((0, 32),), (1, 0, 32, 2.75)),
        "rotation": scatter_about(splits[1], (D, D), 1.0, 6.0, ((0, 32), (1, 8)), jnp.float32),
        "key_weight": gaussian_with(splits[2], (D, F), D ** -0.5, 0.125, ((0, 32), (1, 8)), (0, 1, 32, 2.75)),
        "grad_out": scatter_about(splits[3], (TOKENS, F), 1.0, 6.0, ((0, 32), (1, 8))),
    }


STEP_GAIN = 0.8
LEVELS = 7.0
HIGHEST_PRECISION = lax.Precision.HIGHEST
CONTRACT_ROWS = (((0,), (0,)), ((), ()))
CONTRACT_COLUMNS = (((1,), (1,)), ((), ()))

def soft_quant(entries, peak_value):
    step_size = (peak_value + 1e-05) / LEVELS
    ratios = entries / step_size
    return step_size * (ratios - jnp.sin(2.0 * jnp.pi * ratios) / (2.0 * jnp.pi))

def reference(tokens, rotation, key_weight, grad_out):
    shrink = D ** (-0.5)
    rot_low = rotation.astype(jnp.bfloat16)
    rotated = jnp.dot(tokens, rot_low, preferred_element_type=jnp.float32) * shrink
    token_peak = lax.optimization_barrier(jnp.max(jnp.abs(rotated), axis=1, keepdims=True))
    quant_act = soft_quant(rotated, token_peak).astype(jnp.bfloat16)
    weight_rot = lax.dot_general(key_weight, rot_low, CONTRACT_ROWS, preferred_element_type=jnp.float32) * shrink
    channel_peak = lax.optimization_barrier(jnp.max(jnp.abs(weight_rot), axis=1, keepdims=True))
    quant_weight = soft_quant(weight_rot, channel_peak).astype(jnp.bfloat16)
    projected = lax.dot_general(quant_act, quant_weight, CONTRACT_COLUMNS, preferred_element_type=jnp.float32).astype(jnp.bfloat16)
    grad_act = jnp.dot(grad_out, quant_weight, preferred_element_type=jnp.float32).astype(jnp.bfloat16)
    grad_weight = lax.dot_general(grad_out, quant_act, CONTRACT_ROWS, preferred_element_type=jnp.float32).astype(jnp.bfloat16)
    token_grad = lax.dot_general(tokens, grad_act, CONTRACT_ROWS, preferred_element_type=jnp.float32)
    gradient = (token_grad + jnp.dot(key_weight, grad_weight, preferred_element_type=jnp.float32)) * shrink
    stride = D // PANEL
    panel = rotation[:, ::stride]

    def apply_tangent(block):
        left_part = lax.dot_general(rotation, block, CONTRACT_ROWS, precision=HIGHEST_PRECISION, preferred_element_type=jnp.float32)
        right_part = lax.dot_general(gradient, block, CONTRACT_ROWS, precision=HIGHEST_PRECISION, preferred_element_type=jnp.float32)
        return jnp.dot(gradient, left_part, precision=HIGHEST_PRECISION) - jnp.dot(rotation, right_part, precision=HIGHEST_PRECISION)
    image = apply_tangent(panel)
    alpha = STEP_GAIN * jnp.sqrt(jnp.sum(panel * panel) / (jnp.sum(image * image) + 1e-06))
    updated = panel - alpha * image
    for iteration in range(ITERS):
        updated = panel - 0.5 * alpha * (image + apply_tangent(updated))
    return (projected, updated)
```

```python
import jax
import jax.numpy as jnp
from jax import lax
from jax.sharding import Mesh, PartitionSpec as P

D = 8192
F = 1024
PANEL = 128
STEP_GAIN = 0.8
LEVELS = 7.0

SIZE = {"y": 4, "z": 8, "x": 4, "c": 2}
MP = ("x", "c")
NMP = 8
KA, GA = "y", "z"
NK, NG = SIZE[KA], SIZE[GA]
ROWS = NG * 256
TOKS = NK * 128
COLS = 1024 // NK
SUB = 128 // NG
UNITS = NMP * SUB

LAST = (((1,), (1,)), ((), ()))
bf16, f32 = jnp.bfloat16, jnp.float32


def soft_quant(entries, peak_value):
    step_size = (peak_value + 1e-05) / LEVELS
    ratios = entries / step_size
    return step_size * (ratios - jnp.sin(2.0 * jnp.pi * ratios) / (2.0 * jnp.pi))


def dot(a, b):
    return jnp.dot(a, b, preferred_element_type=f32)


def dot_last(a, b):
    return lax.dot_general(a, b, LAST, preferred_element_type=f32)


def gather(block, axis):
    return lax.all_gather(block, axis, axis=0, tiled=False)


def exchange(blocks, axis):
    return lax.all_to_all(blocks, axis, split_axis=0, concat_axis=0, tiled=True)


def send_all(block, axis):
    n = SIZE[axis]
    return [
        lax.ppermute(block, axis, [(s, (s + k) % n) for s in range(n)]) for k in range(1, n)
    ]


def sum_all(block, axis):
    low = block.astype(bf16)
    total = low.astype(f32)
    for other in send_all(low, axis):
        total = total + other.astype(f32)
    return total


def sum_exact(values, axis):
    total = values
    for other in send_all(values, axis):
        total = total + other
    return total


def sum_with(block, scalars, axis):
    terms = []
    for value in scalars:
        for _ in range(3):
            term = lax.reduce_precision(value, 8, 7)
            terms.append(term)
            value = value - term
    rest = jnp.zeros((16 - len(terms),), f32)
    extra = jnp.broadcast_to(jnp.concatenate([jnp.stack(terms), rest])[:, None], (16, 128))
    total = sum_all(jnp.concatenate([block, extra], 1), axis)
    extra = total[:, -128:]
    sums = [extra[3 * k, 0] + extra[3 * k + 1, 0] + extra[3 * k + 2, 0] for k in range(len(scalars))]
    return total[:, :-128], sums


def body(tokens, rotation, key_weight, grad_out):
    shrink = D ** (-0.5)
    mp = lax.axis_index(MP)
    g = lax.axis_index(GA)

    rot_low = rotation.astype(bf16)
    rot = gather(rot_low, GA).reshape(ROWS, 1024)

    part = lax.dynamic_slice(tokens, (16 * mp, 0), (16, D)).reshape(16, 4, 8, 256)
    part = part.transpose((2, 0, 1, 3) if KA == "z" else (1, 0, 2, 3)).reshape(NK, 16, ROWS)
    tok = gather(exchange(part, KA), MP).reshape(TOKS, ROWS)

    wt = exchange(key_weight.T.reshape(NG, SUB, 256), GA)
    wt = wt.transpose(1, 0, 2).reshape(SUB, ROWS)
    wt = gather(wt, MP).reshape(UNITS, ROWS)

    product = dot(jnp.concatenate([tok, wt], 0), rot).astype(bf16)
    product = product.reshape(TOKS + UNITS, NK, COLS).transpose(1, 0, 2)
    rotated = jnp.sum(exchange(product, KA).astype(f32), axis=0) * shrink
    peak = jnp.max(jnp.abs(rotated), axis=1)
    peak = lax.pmax(lax.pmax(peak, MP), KA)[:, None]
    quant = soft_quant(rotated, peak).astype(bf16)
    quant_act, quant_weight = quant[:TOKS], quant[TOKS:]

    up = gather(grad_out.T, KA)
    up = up.reshape(NK, 128, NMP, 16).transpose(1, 2, 0, 3).reshape(128, TOKS)
    up_all = gather(up, MP).reshape(NMP, NG, SUB, TOKS).transpose(1, 0, 2, 3).reshape(F, TOKS)

    ct = dot(up, tok).astype(bf16).reshape(NG, SUB, ROWS)
    ct = jnp.sum(exchange(ct, GA).astype(f32), axis=0).astype(bf16)
    ct = gather(ct, MP).reshape(UNITS, ROWS)

    gw = dot(up_all, quant_act).astype(bf16).reshape(NG, UNITS, COLS)
    gw = jnp.sum(exchange(gw, GA).astype(f32), axis=0).astype(bf16)
    yk = jnp.concatenate([quant_weight, gw], 0)
    ymat = gather(yk, KA).transpose(1, 0, 2).reshape(2 * UNITS, 1024)
    zt = (dot_last(ymat, rot) * shrink).astype(bf16)
    zt = exchange(zt.reshape(NMP, 2 * UNITS // NMP, ROWS), MP)
    zt = jnp.sum(zt.astype(f32), axis=0).astype(bf16)
    zt = gather(zt, MP).reshape(2 * UNITS, ROWS)

    ut = jnp.concatenate([ct, wt, zt], 0)

    qw_all = gather(quant_weight, GA).reshape(NG, NMP, SUB, COLS).transpose(1, 0, 2, 3)
    projected = dot_last(quant_act, qw_all.reshape(F, COLS)).astype(bf16)
    projected = lax.psum_scatter(projected, MP, scatter_dimension=1, tiled=True)
    projected = projected.reshape(NMP, NK, 16, 128).transpose(1, 0, 2, 3).reshape(TOKS, 128)
    projected = lax.psum_scatter(projected, KA, scatter_dimension=0, tiled=True)

    own = rotation[:, :: D // PANEL].T
    panel = gather(own, GA).transpose(1, 0, 2).reshape(16, ROWS)

    def inner(block):
        return dot_last(block.astype(bf16), ut)

    def outer(v):
        v = v.astype(bf16)
        v = jnp.concatenate([v[:, 2 * UNITS :], -v[:, : 2 * UNITS]], 1)
        return sum_all(dot(v, ut), GA)

    w1 = outer(sum_all(inner(panel), KA))
    v, sums = sum_with(inner(w1), (jnp.sum(panel * panel), jnp.sum(w1 * w1)), KA)
    unit = lax.rsqrt(sums[1] + 1e-06)
    w2 = outer(v * unit)
    totals = jnp.broadcast_to(jnp.stack(sums)[:, None], (2, 128))
    for axis in MP:
        totals = sum_exact(totals, axis)
    alpha = STEP_GAIN * jnp.sqrt(totals[0, 0] / (totals[1, 0] + 1e-06))
    ratio = STEP_GAIN * jnp.sqrt(totals[0, 0] * ((sums[1] + 1e-06) / (totals[1, 0] + 1e-06)))
    w3 = outer(sum_all(inner(w2), KA) * unit)
    step = alpha * (w1 - ratio * (0.5 * w2 - 0.25 * ratio * w3))
    step = lax.dynamic_slice(step, (0, g * 256), (16, 256))
    return projected, (own - step).T


def solution(mesh):
    grid = Mesh(mesh.devices.reshape(4, 8, 4, 2), ("y", "z", "x", "c"))
    dp = ("y", "z")
    placed = (P(dp, None), P(dp, MP), P(dp, MP), P(dp, MP))
    return jax.shard_map(
        body, mesh=grid, in_specs=placed, out_specs=(P(dp, MP), P(dp, MP)), check_vma=False
    )
```

```python
import jax
import jax.numpy as jnp
from jax import lax
from jax.sharding import Mesh, PartitionSpec as P

D = 8192
PANEL = 128
STEP_GAIN = 0.8
LEVELS = 7.0

SIZE = {"y": 4, "z": 8, "x": 4, "c": 2}
MP = ("x", "c")
LAST = (((1,), (1,)), ((), ()))
bf16, f32 = jnp.bfloat16, jnp.float32


def soft_quant(entries, peak_value):
    step_size = (peak_value + 1e-05) / LEVELS
    ratios = entries / step_size
    return step_size * (ratios - jnp.sin(2.0 * jnp.pi * ratios) / (2.0 * jnp.pi))


def dot(a, b):
    return jnp.dot(a, b, preferred_element_type=f32)


def dot_last(a, b):
    return lax.dot_general(a, b, LAST, preferred_element_type=f32)


def shift(block, axis, k):
    n = SIZE[axis]
    return lax.ppermute(block, axis, [(s, (s + k) % n) for s in range(n)])


def other(axis, k):
    return lax.rem(lax.axis_index(axis) + k + SIZE[axis], SIZE[axis])


def piece(array, axis, k, dim):
    size = array.shape[dim] // SIZE[axis]
    return lax.dynamic_slice_in_dim(array, other(axis, k) * size, size, dim)


def pieces(array, axis, dim):
    out = []
    for k in range(SIZE[axis]):
        out.append(piece(array, axis, k, dim))
        array, out[-1] = lax.optimization_barrier((array, out[-1]))
    return out


def place(blocks, axis, dim):
    size, shape = blocks[0].shape[dim], list(blocks[0].shape)
    shape[dim] *= len(blocks)
    out = jnp.zeros(shape, blocks[0].dtype)
    for k, block in enumerate(blocks):
        out = lax.dynamic_update_slice_in_dim(out, block, other(axis, -k) * size, dim)
    return out


def gather(block, axis, dim):
    return place([block] + [shift(block, axis, k) for k in range(1, SIZE[axis])], axis, dim)


def swap(array, axis, dim, to):
    parts = pieces(array, axis, dim)
    return place([parts[0]] + [shift(parts[k], axis, k) for k in range(1, SIZE[axis])], axis, to)


def scatter_sum(array, axis, dim):
    parts = pieces(array, axis, dim)
    total = parts[0].astype(f32)
    for k in range(1, SIZE[axis]):
        total = total + shift(parts[k].astype(bf16), axis, k).astype(f32)
    return total


def sum_all(block, axis):
    low = block.astype(bf16)
    total = low.astype(f32)
    for k in range(1, SIZE[axis]):
        total = total + shift(low, axis, k).astype(f32)
    return total


def sum_z(block):
    low = block.astype(bf16)
    pair = lax.ppermute(low, "z", [(s, s ^ 1) for s in range(8)])
    low = (low.astype(f32) + pair.astype(f32)).astype(bf16)
    total = low.astype(f32)
    for k in (2, 4, 6):
        total = total + shift(low, "z", k).astype(f32)
    return total


def fold_direct(values, axis, op):
    total = values
    for k in range(1, SIZE[axis]):
        total = op(total, shift(values, axis, k))
    return total


def sum_with(block, values, axis):
    lane = lax.broadcasted_iota(jnp.int32, (16, 128), 1)
    extra = jnp.zeros((16, 128), f32)
    for k, value in enumerate(values):
        value = jnp.broadcast_to(value, (16, 128))
        for term in range(3):
            low = lax.reduce_precision(value, 8, 7)
            extra = jnp.where(lane == 3 * k + term, low, extra)
            value = value - low
    total = sum_all(jnp.concatenate([block, extra], 1), axis)
    extra = total[:, -128:]
    return total[:, :-128], [
        jnp.sum(jnp.where((lane >= 3 * k) & (lane < 3 * k + 3), extra, 0.0)) for k in range(len(values))
    ]


def add_pieces(part):
    half = scatter_sum(part, "c", 0)
    return scatter_sum(half, "x", 0).astype(bf16)


def square(block):
    return jnp.sum(block * block, axis=1, keepdims=True)


def whole(block):
    return gather(gather(block, "x", 0), "c", 0)


def body(tokens, rotation, key_weight, grad_out):
    shrink = D ** (-0.5)
    z = lax.axis_index("z")

    rot = lax.all_gather(rotation.astype(bf16), "z", axis=0, tiled=True)

    tok = pieces(tokens, "y", 1)
    tok = jnp.concatenate(tok[:1] + [shift(tok[k], "y", k) for k in range(1, 4)], 0)
    up = jnp.concatenate([grad_out] + [shift(grad_out, "y", k) for k in range(1, 4)], 0).T

    own = rotation[:, :: D // PANEL].T
    sent = jnp.broadcast_to(own.astype(bf16)[None], (8, 16, 256))
    sent = jnp.concatenate([key_weight.T.reshape(8, 16, 256), sent], 1)
    sent = lax.all_to_all(sent, "z", split_axis=0, concat_axis=0, tiled=True)
    sent = sent.transpose(1, 0, 2).reshape(32, 2048)
    panel = sent[16:]
    sent = whole(sent).reshape(8, 2, 16, 2048).transpose(1, 0, 2, 3)
    wt = sent[0].reshape(128, 2048)
    sent = sent.reshape(256, 2048)

    up_all = whole(up).reshape(8, 8, 16, 512).transpose(1, 0, 2, 3).reshape(1024, 512)

    tok, up, up_all, sent, wt, panel, rot = lax.optimization_barrier((tok, up, up_all, sent, wt, panel, rot))
    left = jnp.concatenate([tok, sent], 0)
    blocks = [None] * 4
    for k in (1, 2, 3, 0):
        blocks[k] = dot(left, piece(rot, "y", k, 1))
        if k:
            blocks[k] = shift(blocks[k].astype(bf16), "y", k).astype(f32)
    rows = [
        sum(blocks[d][128 * ((k - d) % 4) : 128 * ((k - d) % 4) + 128] for d in range(4)) for k in range(4)
    ]
    rest = sum(blocks[d][512:] for d in range(4))
    rotated = jnp.concatenate(rows + [rest[:128]], 0) * shrink
    seen = rest[128:].astype(bf16)

    ct = lax.psum_scatter(dot(up, tok).astype(bf16), "z", scatter_dimension=0, tiled=True)

    peak = jnp.max(jnp.abs(rotated), axis=1).reshape(5, 128)
    for axis in ("c", "x"):
        peak = fold_direct(peak, axis, jnp.maximum)
    found = [peak] + [shift(peak, "y", k) for k in range(1, 4)]
    for k in range(1, 4):
        peak = jnp.maximum(peak, jnp.concatenate([found[k][4 - k : 4], found[k][: 4 - k], found[k][4:]], 0))
    quant = soft_quant(rotated, peak.reshape(640, 1)).astype(bf16)
    quant_act, quant_weight = quant[:512], quant[512:]

    gw = dot(up_all, quant_act).astype(bf16).reshape(8, 128, 256)
    gw, quant_weight, seen = lax.optimization_barrier((gw, quant_weight, seen))
    gw = lax.all_to_all(gw, "z", split_axis=0, concat_axis=0, tiled=True)
    both = gather(jnp.concatenate([quant_weight, seen], 0), "y", 1)
    yq, seen = both[:128], both[128:]

    def rotate_back(y):
        part = jnp.concatenate([dot_last(y, rot), dot_last(seen, y)], 1) * shrink
        part = add_pieces(part)
        return part[:, :2048], part[:, 2048:]

    zq, v0q = rotate_back(yq)
    gw = jnp.sum(gw.astype(f32), axis=0).astype(bf16)
    yg = gather(gw, "y", 1)
    zg, v0g = rotate_back(yg)

    base = jnp.concatenate([whole(ct), wt], 0)
    v0 = jnp.concatenate([sum_all(dot_last(panel, base), "y"), v0q.astype(f32), v0g.astype(f32)], 1)
    ut = jnp.concatenate([base, whole(zq), whole(zg)], 0)

    act = [quant_act[128 * k : 128 * k + 128] for k in range(4)]
    act = place([act[0]] + [shift(act[4 - k], "y", k) for k in range(1, 4)], "y", 1)
    qw_all = lax.all_gather(yq, "z", axis=0).reshape(8, 2, 4, 16, 1024).transpose(2, 1, 0, 3, 4).reshape(1024, 1024)
    projected = dot_last(act, qw_all).astype(bf16)

    def inner(block):
        return dot_last(block.astype(bf16), ut)

    def outer(v):
        v = v.astype(bf16)
        return sum_z(dot(jnp.concatenate([v[:, 256:], -v[:, :256]], 1), ut))

    w1 = outer(v0)
    w1, projected = lax.optimization_barrier((w1, projected))
    projected = lax.psum_scatter(projected, MP, scatter_dimension=1, tiled=True)
    wide = panel.astype(f32)
    v, (norm, mine) = sum_with(inner(w1), (square(wide), square(w1)), "y")
    unit = lax.rsqrt(mine + 1e-06)
    w2 = outer(v * unit)
    total = jnp.broadcast_to(jnp.stack([norm, mine])[:, None], (2, 128))
    for axis in ("c", "x"):
        total = fold_direct(total, axis, jnp.add)
    norm, total = total[0, 0], total[1, 0] + 1e-06
    alpha = STEP_GAIN * jnp.sqrt(norm / total)
    ratio = STEP_GAIN * jnp.sqrt(norm * ((mine + 1e-06) / total))
    v = sum_all(inner(w2), "y") * unit
    v, projected = lax.optimization_barrier((v, projected))
    w3 = outer(v)
    step = alpha * (w1 - ratio * (0.5 * w2 - 0.25 * ratio * w3))
    step = lax.dynamic_slice(step, (0, z * 256), (16, 256))
    return projected, (own - step).T


def solution(mesh):
    grid = Mesh(mesh.devices.reshape(4, 8, 4, 2), ("y", "z", "x", "c"))
    dp = ("y", "z")
    placed = (P(dp, None), P(dp, MP), P(dp, MP), P(dp, MP))
    return jax.shard_map(
        body, mesh=grid, in_specs=placed, out_specs=(P(dp, MP), P(dp, MP)), check_vma=False
    )
```

```python
import jax
import jax.numpy as jnp
from jax import lax
from jax.sharding import Mesh, PartitionSpec as P

D = 8192
PANEL = 128
STEP_GAIN = 0.8
LEVELS = 7.0

SIZE = {"y": 4, "z": 8, "x": 4, "c": 2}
MP = ("x", "c")
LAST = (((1,), (1,)), ((), ()))
bf16, f32 = jnp.bfloat16, jnp.float32


def soft_quant(entries, peak_value):
    step_size = (peak_value + 1e-05) / LEVELS
    ratios = entries / step_size
    return step_size * (ratios - jnp.sin(2.0 * jnp.pi * ratios) / (2.0 * jnp.pi))


def dot(a, b):
    return jnp.dot(a, b, preferred_element_type=f32)


def dot_last(a, b):
    return lax.dot_general(a, b, LAST, preferred_element_type=f32)


def shift(block, axis, k):
    n = SIZE[axis]
    return lax.ppermute(block, axis, [(s, (s + k) % n) for s in range(n)])


def other(axis, k):
    return lax.rem(lax.axis_index(axis) + k + SIZE[axis], SIZE[axis])


def piece(array, axis, k, dim):
    size = array.shape[dim] // SIZE[axis]
    return lax.dynamic_slice_in_dim(array, other(axis, k) * size, size, dim)


def pieces(array, axis, dim):
    out = []
    for k in range(SIZE[axis]):
        out.append(piece(array, axis, k, dim))
        array, out[-1] = lax.optimization_barrier((array, out[-1]))
    return out


def place(blocks, axis, dim):
    size, shape = blocks[0].shape[dim], list(blocks[0].shape)
    shape[dim] *= len(blocks)
    out = jnp.zeros(shape, blocks[0].dtype)
    for k, block in enumerate(blocks):
        out = lax.dynamic_update_slice_in_dim(out, block, other(axis, -k) * size, dim)
    return out


def gather(block, axis, dim):
    return place([block] + [shift(block, axis, k) for k in range(1, SIZE[axis])], axis, dim)


def swap(array, axis, dim, to):
    parts = pieces(array, axis, dim)
    return place([parts[0]] + [shift(parts[k], axis, k) for k in range(1, SIZE[axis])], axis, to)


def scatter_sum(array, axis, dim):
    parts = pieces(array, axis, dim)
    total = parts[0].astype(f32)
    for k in range(1, SIZE[axis]):
        total = total + shift(parts[k].astype(bf16), axis, k).astype(f32)
    return total


def sum_all(block, axis):
    low = block.astype(bf16)
    total = low.astype(f32)
    for k in range(1, SIZE[axis]):
        total = total + shift(low, axis, k).astype(f32)
    return total


def sum_z(block, count=0):
    low = block.astype(bf16)
    pair = lax.ppermute(low, "z", [(s, s ^ 1) for s in range(8)])
    low = low.astype(f32) + pair.astype(f32)
    if count:
        low = jnp.concatenate([low[:, :-128], split(join(low[:, -128:], count))], 1)
    low = low.astype(bf16)
    total = low.astype(f32)
    for k in (2, 4, 6):
        total = total + shift(low, "z", k).astype(f32)
    return total


def fold_direct(values, axis, op):
    total = values
    for k in range(1, SIZE[axis]):
        total = op(total, shift(values, axis, k))
    return total


def split(values):
    lane = lax.broadcasted_iota(jnp.int32, (16, 128), 1)
    extra = jnp.zeros((16, 128), f32)
    for k, value in enumerate(values):
        value = jnp.broadcast_to(value, (16, 128))
        for term in range(3):
            low = lax.reduce_precision(value, 8, 7)
            extra = jnp.where(lane == 3 * k + term, low, extra)
            value = value - low
    return extra


def join(extra, count):
    lane = lax.broadcasted_iota(jnp.int32, (16, 128), 1)
    return [
        jnp.sum(jnp.where((lane >= 3 * k) & (lane < 3 * k + 3), extra, 0.0), axis=1, keepdims=True)
        for k in range(count)
    ]


def add_pieces(part):
    half = scatter_sum(part, "c", 1)
    return scatter_sum(half, "x", 1).astype(bf16)


def square(block):
    return jnp.sum(block * block, axis=1, keepdims=True)


def whole(block):
    return gather(gather(block, "x", 0), "c", 0)


def body(tokens, rotation, key_weight, grad_out):
    shrink = D ** (-0.5)
    z = lax.axis_index("z")

    rot = lax.all_gather(rotation.astype(bf16), "z", axis=0, tiled=True)

    tok = pieces(tokens, "y", 1)
    tok = jnp.concatenate(tok[:1] + [shift(tok[k], "y", k) for k in range(1, 4)], 0)
    up = jnp.concatenate([grad_out] + [shift(grad_out, "y", k) for k in range(1, 4)], 0).T

    own = rotation[:, :: D // PANEL].T
    sent = jnp.broadcast_to(own.astype(bf16)[None], (8, 16, 256))
    sent = jnp.concatenate([key_weight.T.reshape(8, 16, 256), sent], 1)
    sent = lax.all_to_all(sent, "z", split_axis=0, concat_axis=0, tiled=True)
    sent = sent.transpose(1, 0, 2).reshape(32, 2048)
    panel = sent[16:]
    sent = whole(sent).reshape(8, 2, 16, 2048).transpose(1, 0, 2, 3)
    wt = sent[0].reshape(128, 2048)
    sent = sent.reshape(256, 2048)

    up_all = whole(up).reshape(8, 8, 16, 512).transpose(1, 0, 2, 3).reshape(1024, 512)

    tok, up, up_all, sent, wt, panel, rot = lax.optimization_barrier((tok, up, up_all, sent, wt, panel, rot))
    left = jnp.concatenate([tok, sent], 0)
    blocks = [None] * 4
    for k in (1, 2, 3, 0):
        blocks[k] = dot(left, piece(rot, "y", k, 1))
        if k:
            blocks[k] = shift(blocks[k].astype(bf16), "y", k).astype(f32)
    rows = [
        sum(blocks[d][128 * ((k - d) % 4) : 128 * ((k - d) % 4) + 128] for d in range(4)) for k in range(4)
    ]
    rest = sum(blocks[d][512:] for d in range(4))
    rotated = jnp.concatenate(rows + [rest[:128]], 0) * shrink
    seen = rest[128:].astype(bf16)

    ct = lax.psum_scatter(dot(up, tok).astype(bf16), "z", scatter_dimension=0, tiled=True)

    peak = jnp.max(jnp.abs(rotated), axis=1).reshape(5, 128)
    for axis in ("c", "x"):
        peak = fold_direct(peak, axis, jnp.maximum)
    found = [peak] + [shift(peak, "y", k) for k in range(1, 4)]
    for k in range(1, 4):
        peak = jnp.maximum(peak, jnp.concatenate([found[k][4 - k : 4], found[k][: 4 - k], found[k][4:]], 0))
    quant = soft_quant(rotated, peak.reshape(640, 1)).astype(bf16)
    quant_act, quant_weight = quant[:512], quant[512:]

    choose = 64 * lax.broadcasted_iota(jnp.int32, (16, 256), 0) == lax.broadcasted_iota(jnp.int32, (16, 256), 1)
    mine = dot_last(choose.astype(bf16), rotated.astype(bf16)).astype(bf16)
    first = dot_last(mine[:, :512], up_all).astype(bf16).reshape(16, 8, 128).transpose(1, 0, 2)
    second = mine[:, 512:]
    first = jnp.concatenate([first, jnp.zeros((8, 16, 128), bf16)], 2)

    gw = dot(up_all, quant_act).astype(bf16).reshape(8, 128, 256)
    gw = jnp.concatenate([gw, first], 1)
    gw, quant_act, quant_weight, seen = lax.optimization_barrier((gw, quant_act, quant_weight, seen))
    gw = lax.all_to_all(gw, "z", split_axis=0, concat_axis=0, tiled=True)
    both = gather(jnp.concatenate([quant_weight, seen], 0), "y", 1)
    yq, seen = both[:128], both[128:]
    act = [quant_act[128 * k : 128 * k + 128] for k in range(4)]
    act = place([act[0]] + [shift(act[4 - k], "y", k) for k in range(1, 4)], "y", 1)
    ut = jnp.concatenate([wt[None], jnp.zeros((3, 128, 2048), bf16)], 0)
    gw, yq, seen, act, ut = lax.optimization_barrier((gw, yq, seen, act, ut))

    gw = jnp.sum(gw.astype(f32), axis=0).astype(bf16)
    gw = jnp.concatenate([gw[:128], jnp.concatenate([gw[128:, :128], second], 1)], 0)
    found = [gw] + [shift(gw, "y", k) for k in range(1, 4)]
    yg = place([block[:128] for block in found], "y", 1)
    v0 = place([block[128:132].astype(f32) for block in found], "y", 0) * (1.0 / shrink)

    back = (dot_last(jnp.concatenate([yq, yg], 0), rot) * shrink).astype(bf16).reshape(2, 128, 2048)
    seen = (jnp.stack([dot_last(seen, yq), dot_last(seen, yg)]) * shrink).astype(bf16)
    part = add_pieces(jnp.concatenate([back, seen], 2))
    v0 = jnp.concatenate([v0[:, 128:], v0[:, :128], part[0, :, 2048:].astype(f32), part[1, :, 2048:].astype(f32)], 1)
    half = gather(jnp.concatenate([ct[None], part[:, :, :2048]], 0), "x", 1)
    c = lax.axis_index("c")
    ut = lax.dynamic_update_slice(ut, half, (1, 64 * c, 0))
    ut = lax.dynamic_update_slice(ut, shift(half, "c", 1), (1, 64 * (1 - c), 0)).reshape(512, 2048)

    qw_all = lax.all_gather(yq, "z", axis=0).reshape(1024, 1024)
    projected = dot_last(qw_all, act).astype(bf16).reshape(8, 2, 4, 16, 128)
    projected = projected.transpose(2, 1, 0, 3, 4).reshape(1024, 128)

    def inner(block):
        return dot_last(block.astype(bf16), ut)

    def outer(v):
        v = v.astype(bf16)
        return dot(jnp.concatenate([v[:, 384:], v[:, 256:384], -v[:, 128:256], -v[:, :128]], 1), ut)

    w1 = sum_z(outer(v0))
    w1, projected = lax.optimization_barrier((w1, projected))
    projected = lax.all_to_all(projected.reshape(8, 128, 128), MP, split_axis=0, concat_axis=0, tiled=True)
    projected = jnp.sum(projected.astype(f32), axis=0).astype(bf16)

    wide = panel.astype(f32)
    v = sum_all(jnp.concatenate([inner(w1), split((square(wide), square(w1)))], 1), "y")
    sums = jnp.concatenate(join(v[:, 512:], 2), 1)
    norm, mine = jnp.sum(sums[:, 0]), jnp.sum(sums[:, 1])
    unit = lax.rsqrt(mine + 1e-06)
    w2 = sum_z(outer(v[:, :512] * unit))
    total = jnp.broadcast_to(jnp.stack([norm, mine])[:, None], (2, 128))
    for axis in ("c", "x"):
        total = fold_direct(total, axis, jnp.add)
    w2, total = lax.optimization_barrier((w2, total))
    v = sum_all(inner(w2), "y") * unit
    v, projected = lax.optimization_barrier((v, projected))
    w3 = sum_z(outer(v))
    norm, total = total[0, 0], total[1, 0]
    total = total + 1e-06
    alpha = STEP_GAIN * jnp.sqrt(norm / total)
    ratio = STEP_GAIN * jnp.sqrt(norm * ((mine + 1e-06) / total))
    step = alpha * (w1 - ratio * (0.5 * w2 - 0.25 * ratio * w3))
    step = lax.dynamic_slice(step, (0, z * 256), (16, 256))
    return projected.T, (own - step).T


def solution(mesh):
    grid = Mesh(mesh.devices.reshape(4, 8, 4, 2), ("y", "z", "x", "c"))
    dp = ("y", "z")
    placed = (P(dp, None), P(dp, MP), P(dp, MP), P(dp, MP))
    return jax.shard_map(
        body, mesh=grid, in_specs=placed, out_specs=(P(dp, MP), P(dp, MP)), check_vma=False
    )
```

```python
import jax
import jax.numpy as jnp
from jax import lax
from jax.sharding import Mesh, PartitionSpec as P

D = 8192
PANEL = 128
STEP_GAIN = 0.8
LEVELS = 7.0

SIZE = {"y": 4, "z": 8, "x": 4, "c": 2}
MP = ("x", "c")
LAST = (((1,), (1,)), ((), ()))
bf16, f32 = jnp.bfloat16, jnp.float32


def soft_quant(entries, peak_value):
    step_size = (peak_value + 1e-05) / LEVELS
    ratios = entries / step_size
    return step_size * (ratios - jnp.sin(2.0 * jnp.pi * ratios) / (2.0 * jnp.pi))


def dot(a, b):
    return jnp.dot(a, b, preferred_element_type=f32)


def dot_last(a, b):
    return lax.dot_general(a, b, LAST, preferred_element_type=f32)


def shift(block, axis, k):
    n = SIZE[axis]
    return lax.ppermute(block, axis, [(s, (s + k) % n) for s in range(n)])


def other(axis, k):
    return lax.rem(lax.axis_index(axis) + k + SIZE[axis], SIZE[axis])


def piece(array, axis, k, dim):
    size = array.shape[dim] // SIZE[axis]
    return lax.dynamic_slice_in_dim(array, other(axis, k) * size, size, dim)


def pieces(array, axis, dim):
    out = []
    for k in range(SIZE[axis]):
        out.append(piece(array, axis, k, dim))
        array, out[-1] = lax.optimization_barrier((array, out[-1]))
    return out


def place(blocks, axis, dim):
    size, shape = blocks[0].shape[dim], list(blocks[0].shape)
    shape[dim] *= len(blocks)
    out = jnp.zeros(shape, blocks[0].dtype)
    for k, block in enumerate(blocks):
        out = lax.dynamic_update_slice_in_dim(out, block, other(axis, -k) * size, dim)
    return out


def gather(block, axis, dim):
    return place([block] + [shift(block, axis, k) for k in range(1, SIZE[axis])], axis, dim)


def swap(array, axis, dim, to):
    parts = pieces(array, axis, dim)
    return place([parts[0]] + [shift(parts[k], axis, k) for k in range(1, SIZE[axis])], axis, to)


def scatter_sum(array, axis, dim):
    parts = pieces(array, axis, dim)
    total = parts[0].astype(f32)
    for k in range(1, SIZE[axis]):
        total = total + shift(parts[k].astype(bf16), axis, k).astype(f32)
    return total


def sum_all(block, axis):
    low = block.astype(bf16)
    total = low.astype(f32)
    for k in range(1, SIZE[axis]):
        total = total + shift(low, axis, k).astype(f32)
    return total


def sum_z(block, count=0):
    low = block.astype(bf16)
    pair = lax.ppermute(low, "z", [(s, s ^ 1) for s in range(8)])
    low = low.astype(f32) + pair.astype(f32)
    if count:
        low = jnp.concatenate([low[:, :-128], split(join(low[:, -128:], count))], 1)
    low = low.astype(bf16)
    total = low.astype(f32)
    for k in (2, 4, 6):
        total = total + shift(low, "z", k).astype(f32)
    return total


def fold_direct(values, axis, op):
    total = values
    for k in range(1, SIZE[axis]):
        total = op(total, shift(values, axis, k))
    return total


def split(values):
    lane = lax.broadcasted_iota(jnp.int32, (16, 128), 1)
    extra = jnp.zeros((16, 128), f32)
    for k, value in enumerate(values):
        value = jnp.broadcast_to(value, (16, 128))
        for term in range(3):
            low = lax.reduce_precision(value, 8, 7)
            extra = jnp.where(lane == 3 * k + term, low, extra)
            value = value - low
    return extra


def join(extra, count):
    lane = lax.broadcasted_iota(jnp.int32, (16, 128), 1)
    return [
        jnp.sum(jnp.where((lane >= 3 * k) & (lane < 3 * k + 3), extra, 0.0), axis=1, keepdims=True)
        for k in range(count)
    ]


def add_pieces(part):
    half = scatter_sum(part, "c", 1)
    return scatter_sum(half, "x", 1).astype(bf16)


def square(block):
    return jnp.sum(block * block, axis=1, keepdims=True)


def whole(block):
    return gather(gather(block, "x", 0), "c", 0)


def body(tokens, rotation, key_weight, grad_out):
    shrink = D ** (-0.5)
    z = lax.axis_index("z")

    rot = lax.all_gather(rotation.astype(bf16), "z", axis=0, tiled=True)

    tok = pieces(tokens, "y", 1)
    tok = jnp.concatenate(tok[:1] + [shift(tok[k], "y", k) for k in range(1, 4)], 0)
    up = jnp.concatenate([grad_out] + [shift(grad_out, "y", k) for k in range(1, 4)], 0).T

    own = rotation[:, :: D // PANEL].T
    sent = jnp.broadcast_to(own.astype(bf16)[None], (8, 16, 256))
    sent = jnp.concatenate([key_weight.T.reshape(8, 16, 256), sent], 1)
    sent = lax.all_to_all(sent, "z", split_axis=0, concat_axis=0, tiled=True)
    sent = sent.transpose(1, 0, 2).reshape(32, 2048)
    panel = sent[16:]
    sent = whole(sent).reshape(8, 2, 16, 2048).transpose(1, 0, 2, 3)
    wt = sent[0].reshape(128, 2048)
    sent = sent.reshape(256, 2048)

    up_all = whole(up).reshape(8, 8, 16, 512).transpose(1, 0, 2, 3).reshape(1024, 512)

    tok, up, up_all, sent, wt, panel, rot = lax.optimization_barrier((tok, up, up_all, sent, wt, panel, rot))
    left = jnp.concatenate([tok, sent], 0)
    blocks = [None] * 4
    for k in (1, 2, 3, 0):
        blocks[k] = dot(left, piece(rot, "y", k, 1))
        if k:
            blocks[k] = shift(blocks[k].astype(bf16), "y", k).astype(f32)
    rows = [
        sum(blocks[d][128 * ((k - d) % 4) : 128 * ((k - d) % 4) + 128] for d in range(4)) for k in range(4)
    ]
    rest = sum(blocks[d][512:] for d in range(4))
    rotated = jnp.concatenate(rows + [rest[:128]], 0) * shrink
    seen = rest[128:].astype(bf16)

    ct = lax.psum_scatter(dot(up, tok).astype(bf16), "z", scatter_dimension=0, tiled=True)

    peak = jnp.max(jnp.abs(rotated), axis=1).reshape(5, 128)
    for axis in ("c", "x"):
        peak = fold_direct(peak, axis, jnp.maximum)
    found = [peak] + [shift(peak, "y", k) for k in range(1, 4)]
    for k in range(1, 4):
        peak = jnp.maximum(peak, jnp.concatenate([found[k][4 - k : 4], found[k][: 4 - k], found[k][4:]], 0))
    quant = soft_quant(rotated, peak.reshape(640, 1)).astype(bf16)
    quant_act, quant_weight = quant[:512], quant[512:]

    choose = 64 * lax.broadcasted_iota(jnp.int32, (16, 256), 0) == lax.broadcasted_iota(jnp.int32, (16, 256), 1)
    mine = dot_last(choose.astype(bf16), rotated.astype(bf16)).astype(bf16)
    first = dot_last(mine[:, :512], up_all).astype(bf16).reshape(16, 8, 128).transpose(1, 0, 2)
    second = mine[:, 512:]
    first = jnp.concatenate([first, jnp.zeros((8, 16, 128), bf16)], 2)

    gw = dot(up_all, quant_act).astype(bf16).reshape(8, 128, 256)
    gw = jnp.concatenate([gw, first], 1)
    gw, quant_act, quant_weight, seen = lax.optimization_barrier((gw, quant_act, quant_weight, seen))
    gw = lax.all_to_all(gw, "z", split_axis=0, concat_axis=0, tiled=True)
    both = gather(jnp.concatenate([quant_weight, seen], 0), "y", 1)
    yq, seen = both[:128], both[128:]
    act = [quant_act[128 * k : 128 * k + 128] for k in range(4)]
    act = place([act[0]] + [shift(act[4 - k], "y", k) for k in range(1, 4)], "y", 1)
    ut = jnp.concatenate([wt[None], jnp.zeros((3, 128, 2048), bf16)], 0)
    gw, yq, seen, act, ut = lax.optimization_barrier((gw, yq, seen, act, ut))

    gw = jnp.sum(gw.astype(f32), axis=0).astype(bf16)
    gw = jnp.concatenate([gw[:128], jnp.concatenate([gw[128:, :128], second], 1)], 0)
    found = [gw] + [shift(gw, "y", k) for k in range(1, 4)]
    yg = place([block[:128] for block in found], "y", 1)
    v0 = place([block[128:132].astype(f32) for block in found], "y", 0) * (1.0 / shrink)

    back = (dot_last(jnp.concatenate([yq, yg], 0), rot) * shrink).astype(bf16).reshape(2, 128, 2048)
    seen = (jnp.stack([dot_last(seen, yq), dot_last(seen, yg)]) * shrink).astype(bf16)
    part = add_pieces(jnp.concatenate([back, seen], 2))
    v0 = jnp.concatenate([v0[:, 128:], v0[:, :128], part[0, :, 2048:].astype(f32), part[1, :, 2048:].astype(f32)], 1)
    half = gather(jnp.concatenate([ct[None], part[:, :, :2048]], 0), "x", 1)
    c = lax.axis_index("c")
    ut = lax.dynamic_update_slice(ut, half, (1, 64 * c, 0))
    ut = lax.dynamic_update_slice(ut, shift(half, "c", 1), (1, 64 * (1 - c), 0)).reshape(512, 2048)

    qw_all = lax.all_gather(yq, "z", axis=0).reshape(1024, 1024)
    projected = dot_last(qw_all, act).astype(bf16).reshape(8, 2, 4, 16, 128)
    projected = projected.transpose(2, 1, 0, 3, 4).reshape(1024, 128)

    def inner(block):
        return dot_last(block.astype(bf16), ut)

    def outer(v):
        v = v.astype(bf16)
        return dot(jnp.concatenate([v[:, 384:], v[:, 256:384], -v[:, 128:256], -v[:, :128]], 1), ut)

    w1 = sum_z(outer(v0))
    w1, projected = lax.optimization_barrier((w1, projected))
    projected = lax.all_to_all(projected.reshape(8, 128, 128), MP, split_axis=0, concat_axis=0, tiled=True)
    projected = jnp.sum(projected.astype(f32), axis=0).astype(bf16)

    wide = panel.astype(f32)
    v = sum_all(jnp.concatenate([inner(w1), split((square(wide), square(w1)))], 1), "y")
    sums = jnp.concatenate(join(v[:, 512:], 2), 1)
    norm, mine = jnp.sum(sums[:, 0]), jnp.sum(sums[:, 1])
    unit = lax.rsqrt(mine + 1e-06)
    w2 = sum_z(outer(v[:, :512] * unit))
    total = jnp.broadcast_to(jnp.stack([norm, mine])[:, None], (2, 128))
    for axis in ("c", "x"):
        total = fold_direct(total, axis, jnp.add)
    w2, total, projected = lax.optimization_barrier((w2, total, projected))
    v = sum_all(inner(w2), "y") * unit
    w3 = sum_z(outer(v))
    norm, total = total[0, 0], total[1, 0]
    total = total + 1e-06
    alpha = STEP_GAIN * jnp.sqrt(norm / total)
    ratio = STEP_GAIN * jnp.sqrt(norm * ((mine + 1e-06) / total))
    step = alpha * (w1 - ratio * (0.5 * w2 - 0.25 * ratio * w3))
    step = lax.dynamic_slice(step, (0, z * 256), (16, 256))
    return projected.T, (own - step).T


def solution(mesh):
    grid = Mesh(mesh.devices.reshape(4, 8, 4, 2), ("y", "z", "x", "c"))
    dp = ("y", "z")
    placed = (P(dp, None), P(dp, MP), P(dp, MP), P(dp, MP))
    return jax.shard_map(
        body, mesh=grid, in_specs=placed, out_specs=(P(dp, MP), P(dp, MP)), check_vma=False
    )
```
